32 devices in a mesh: ctx: 8 (over z, y), head: 4 (over x, core).
Axes of the slice: x: 2, y: 2, z: 4, core: 2. Of those that a mesh axis runs over, the one named last changes fastest.
Arguments:
- tokens: bfloat16 [3072, 3840], P(('ctx', 'head'))
- w_query: bfloat16 [3840, 4096], P(None, 'head')
- w_key: bfloat16 [3840, 2048], P(None, 'head')
- w_value: bfloat16 [3840, 2048], P(None, 'head'), may hold values from -0.09375 to 0.09375
- query_gain: float32 [256], replicated
- key_gain: float32 [256], replicated
- positions: int32 [3072], P('ctx'), may hold values from 0 to 3071, as said below
- out_grad: bfloat16 [3072, 4096], P('ctx', 'head'), may hold values from -6 to 6
Outputs:
- attended: bfloat16 [3072, 4096], P('ctx', 'head')
- input_grad: bfloat16 [3072, 3840], P(('ctx', 'head'))
- grad_query: bfloat16 [3840, 4096], P('ctx', 'head')
- grad_key: bfloat16 [3840, 2048], P('ctx', 'head')
- grad_value: bfloat16 [3840, 2048], P('ctx', 'head')
The draws below stay inside these ranges and needn't reach their ends.
Inputs may be any that keep to these rules, and one draw needn't show every extreme that they name: `positions`: positions rise by one from token to token inside a document and are 0 at a document's first token; the window's first document began before the window; no document that starts inside the window is longer than 2048 tokens.
All inputs are finite; a program needn't handle non-finite values.
Results may differ from the reference program's by a relative error of at most 0.04.
The reference program's roundings to bfloat16 on the way count: a program that leaves them out, or rounds other values in their place, can miss the bound.
Values may be sent and summed in bfloat16 or wider, within the bound.
A program may use at most 192 MiB of HBM per device.

```python
import math
import jax
import jax.numpy as jnp
from jax import lax

D = 3840
HEADS = 16
KV_HEADS = 8
HEAD_DIM = 256
WINDOW = 1024
TOK_DEV = 384
TOKENS = 3072
REACH = 3
PROJ = 8192
N_CTX = 8


def draw_tokens(key, part):
    draws = jnp.clip(jax.random.normal(jax.random.fold_in(key, 3), (TOKENS, D), jnp.float32), -6.0, 6.0)
    return draws.astype(jnp.bfloat16)


def draw_w_query(key, part):
    random_part = jax.random.normal(jax.random.fold_in(key, 1), (D, HEADS, HEAD_DIM), jnp.float32)
    return (random_part / jnp.sqrt(float(D))).reshape(D, HEADS * HEAD_DIM).astype(jnp.bfloat16)


def draw_w_key(key, part):
    random_part = jax.random.normal(jax.random.fold_in(key, 2), (D, KV_HEADS, HEAD_DIM), jnp.float32)
    return (random_part / jnp.sqrt(float(D))).reshape(D, KV_HEADS * HEAD_DIM).astype(jnp.bfloat16)


def draw_query_gain(key, part):
    return jnp.exp(jax.random.uniform(jax.random.fold_in(key, 21), (HEAD_DIM,), jnp.float32, 0.0, 0.92))


def draw_key_gain(key, part):
    return jnp.exp(jax.random.uniform(jax.random.fold_in(key, 22), (HEAD_DIM,), jnp.float32, 0.0, 0.92))


def draw_positions(key, part):
    token_index = jnp.arange(TOKENS, dtype=jnp.int32)
    random_start = jax.random.randint(jax.random.fold_in(key, 5), (TOKENS,), 0, WINDOW) == 0
    after_first = token_index - WINDOW
    forced_start = (after_first >= 0) & (after_first % (2 * WINDOW) == 0)
    boundary = forced_start | random_start & (after_first > 0)
    last_start = lax.cummax(jnp.where(boundary, token_index, -2 * WINDOW), axis=0)
    return (token_index - last_start).astype(jnp.int32)


def level_of(stream_key, extent, pieces, least, largest):
    loudness, own = 1.0, jax.random.fold_in(stream_key, 6)
    for dim, shards_of in pieces:
        steps = jnp.exp(jax.random.uniform(jax.random.fold_in(own, dim), (shards_of,), jnp.float32, least / len(pieces), largest / len(pieces)))
        loudness = loudness * jnp.repeat(steps, extent[dim] // shards_of).reshape([-1 if axis == dim else 1 for axis in range(len(extent))])
    return loudness


def bell_draw(key, dims, spread, bound, cuts=(), held_as=jnp.bfloat16):
    result = jax.random.normal(key, dims, jnp.float32) * spread
    if len(cuts) > 0:
        result = level_of(key, dims, cuts, -0.22, 0.18) * result
    return jnp.clip(result, min=-bound, max=bound).astype(held_as)


def setup_inputs(seed: int = 0) -> dict:
    streams_of = jax.random.split(jax.random.key(seed), 9)
    tokens = draw_tokens(jax.random.fold_in(streams_of[8], 71), 0)
    w_query = draw_w_query(jax.random.fold_in(streams_of[8], 71), 0)
    w_key = draw_w_key(jax.random.fold_in(streams_of[8], 71), 0)
    w_value = bell_draw(streams_of[3], (D, KV_HEADS * HEAD_DIM), D ** -0.5, 0.09375, ((1, 4),))
    query_gain = draw_query_gain(jax.random.fold_in(streams_of[8], 71), 0)
    key_gain = draw_key_gain(jax.random.fold_in(streams_of[8], 71), 0)
    positions = draw_positions(jax.random.fold_in(streams_of[8], 71), 0)
    out_grad = bell_draw(streams_of[7], (TOKENS, HEADS * HEAD_DIM), 1.0, 6.0, ((0, 8), (1, 4)))
    return {"tokens": tokens, "w_query": w_query, "w_key": w_key, "w_value": w_value, "query_gain": query_gain, "key_gain": key_gain, "positions": positions, "out_grad": out_grad}


norm_eps = 1e-06
rope_base = 10000.0

def rope_tables(positions, head_width):
    half_width = head_width // 2
    indices = jnp.arange(half_width, dtype=jnp.float32)
    frequency = jnp.power(rope_base, -2.0 * indices / head_width)
    angles = positions.astype(jnp.float32)[:, None] * frequency[None, :]
    return (jnp.cos(angles)[:, None, :], jnp.sin(angles)[:, None, :])

def rotate(vector, cosine_table, sine_table):
    half_width = vector.shape[-1] // 2
    lower_half = vector[..., :half_width]
    upper_half = vector[..., half_width:]
    return jnp.concatenate([lower_half * cosine_table - upper_half * sine_table, upper_half * cosine_table + lower_half * sine_table], axis=-1)

def unrotate(rotated, cosine_table, sine_table):
    half_width = rotated.shape[-1] // 2
    lower_half = rotated[..., :half_width]
    upper_half = rotated[..., half_width:]
    return jnp.concatenate([lower_half * cosine_table + upper_half * sine_table, upper_half * cosine_table - lower_half * sine_table], axis=-1)

def normalize(vector, gain_vector):
    inv_rms = lax.rsqrt(lax.optimization_barrier(jnp.mean(vector * vector, axis=-1, keepdims=True)) + norm_eps)
    return (vector * inv_rms * gain_vector, inv_rms)

def norm_back(vector, inv_rms, gain_vector, upstream):
    scaled = upstream * gain_vector
    return inv_rms * scaled - vector * (inv_rms * inv_rms * inv_rms) * lax.optimization_barrier(jnp.mean(vector * scaled, axis=-1, keepdims=True))

def through_bf16(vector):
    return lax.optimization_barrier(vector.astype(jnp.bfloat16)).astype(jnp.float32)

def reference(tokens, w_query, w_key, w_value, query_gain, key_gain, positions, out_grad):
    group_size = HEADS // KV_HEADS
    query_scale = 1.0 / math.sqrt(HEAD_DIM)
    query_raw = jnp.dot(tokens, w_query, preferred_element_type=jnp.float32).reshape(TOKENS, HEADS, HEAD_DIM)
    key_raw = jnp.dot(tokens, w_key, preferred_element_type=jnp.float32).reshape(TOKENS, KV_HEADS, HEAD_DIM)
    value_states = jnp.dot(tokens, w_value, preferred_element_type=jnp.float32).astype(jnp.bfloat16).reshape(TOKENS, KV_HEADS, HEAD_DIM)
    cosine_table, sine_table = rope_tables(positions, HEAD_DIM)
    query_normed, query_inv = normalize(query_raw, query_gain)
    key_normed, key_inv = normalize(key_raw, key_gain)
    query_states = (rotate(query_normed, cosine_table, sine_table) * query_scale).astype(jnp.bfloat16)
    key_states = rotate(key_normed, cosine_table, sine_table).astype(jnp.bfloat16)
    pad_rows = REACH * TOK_DEV
    key_span = (REACH + 1) * TOK_DEV
    key_padded = jnp.concatenate([jnp.zeros((pad_rows, KV_HEADS, HEAD_DIM), jnp.bfloat16), key_states], axis=0)
    value_padded = jnp.concatenate([jnp.zeros((pad_rows, KV_HEADS, HEAD_DIM), jnp.bfloat16), value_states], axis=0)
    query_blocks = query_states.reshape(N_CTX, TOK_DEV, KV_HEADS, group_size, HEAD_DIM)
    grad_blocks = out_grad.reshape(N_CTX, TOK_DEV, KV_HEADS, group_size, HEAD_DIM)
    position_blocks = positions.reshape(N_CTX, TOK_DEV)
    query_offsets = jnp.arange(TOK_DEV, dtype=jnp.int32)
    key_offsets = jnp.arange(key_span, dtype=jnp.int32)

    def attend_block(accumulated, operands):
        key_grad_sum, value_grad_sum = accumulated
        block_index, query_block, grad_block, position_block = operands
        first_row = block_index * TOK_DEV
        key_block = lax.dynamic_slice_in_dim(key_padded, first_row, key_span, 0).astype(jnp.float32)
        value_block = lax.dynamic_slice_in_dim(value_padded, first_row, key_span, 0).astype(jnp.float32)
        query_index = first_row + query_offsets
        key_index = first_row - pad_rows + key_offsets
        distance = query_index[:, None] - key_index[None, :]
        reach_limit = jnp.minimum(position_block, WINDOW - 1)[:, None]
        visible = (distance >= 0) & (distance <= reach_limit) & (key_index[None, :] >= 0)
        query_float = query_block.astype(jnp.float32)
        grad_float = grad_block.astype(jnp.float32)
        scores = jnp.einsum('qgue,kge->guqk', query_float, key_block)
        row_peak = lax.optimization_barrier(jnp.max(jnp.where(visible, scores, -jnp.inf), axis=-1, keepdims=True))
        weights = jnp.where(visible, jnp.exp(scores - row_peak), 0.0)
        probabilities = weights / lax.optimization_barrier(jnp.sum(weights, axis=-1, keepdims=True))
        prob_float = through_bf16(probabilities)
        attended = jnp.einsum('guqk,kge->qgue', prob_float, value_block)
        attended_bf = attended.astype(jnp.bfloat16)
        attended_float = lax.optimization_barrier(attended_bf).astype(jnp.float32)
        row_delta = jnp.einsum('qgue,qgue->guq', grad_float, attended_float)[..., None]
        dprobs = jnp.einsum('qgue,kge->guqk', grad_float, value_block)
        dscores = through_bf16(probabilities * (dprobs - row_delta))
        query_grad = jnp.einsum('guqk,kge->qgue', dscores, key_block)
        key_grad = jnp.einsum('guqk,qgue->kge', dscores, query_float)
        value_grad = jnp.einsum('guqk,qgue->kge', prob_float, grad_float)
        key_grad_sum = lax.dynamic_update_slice_in_dim(key_grad_sum, lax.dynamic_slice_in_dim(key_grad_sum, first_row, key_span, 0) + key_grad, first_row, 0)
        value_grad_sum = lax.dynamic_update_slice_in_dim(value_grad_sum, lax.dynamic_slice_in_dim(value_grad_sum, first_row, key_span, 0) + value_grad, first_row, 0)
        return ((key_grad_sum, value_grad_sum), (attended_bf, query_grad))
    zero_sum = jnp.zeros((pad_rows + TOKENS, KV_HEADS, HEAD_DIM), jnp.float32)
    block_ids = jnp.arange(N_CTX, dtype=jnp.int32)
    sums, outputs = lax.scan(attend_block, (zero_sum, zero_sum), (block_ids, query_blocks, grad_blocks, position_blocks))
    key_grad_sum, value_grad_sum = sums
    attended_blocks, query_grad_blocks = outputs
    attended = attended_blocks.reshape(TOKENS, HEADS * HEAD_DIM)
    query_grads = query_grad_blocks.reshape(TOKENS, HEADS, HEAD_DIM)
    key_grads = key_grad_sum[pad_rows:]
    value_grads = value_grad_sum[pad_rows:].astype(jnp.bfloat16).reshape(TOKENS, KV_HEADS * HEAD_DIM)
    query_raw_grad = norm_back(query_raw, query_inv, query_gain, unrotate(query_grads, cosine_table, sine_table) * query_scale).astype(jnp.bfloat16).reshape(TOKENS, HEADS * HEAD_DIM)
    key_raw_grad = norm_back(key_raw, key_inv, key_gain, unrotate(key_grads, cosine_table, sine_table)).astype(jnp.bfloat16).reshape(TOKENS, KV_HEADS * HEAD_DIM)
    input_grad = (jnp.dot(query_raw_grad, w_query.T, preferred_element_type=jnp.float32) + jnp.dot(key_raw_grad, w_key.T, preferred_element_type=jnp.float32) + jnp.dot(value_grads, w_value.T, preferred_element_type=jnp.float32)).astype(jnp.bfloat16)
    grad_columns = jnp.concatenate([query_raw_grad, key_raw_grad, value_grads], axis=1)
    token_blocks = tokens.reshape(N_CTX, TOK_DEV, D)
    column_blocks = grad_columns.reshape(N_CTX, TOK_DEV, PROJ)

    def add_term(weight_sum, operands):
        block_term = jnp.dot(operands[0].T, operands[1], preferred_element_type=jnp.float32)
        return (weight_sum + through_bf16(block_term), None)
    weight_sum, unused = lax.scan(add_term, jnp.zeros((D, PROJ), jnp.float32), (token_blocks, column_blocks))
    query_cols = HEADS * HEAD_DIM
    key_cols = KV_HEADS * HEAD_DIM
    grad_query = weight_sum[:, :query_cols].astype(jnp.bfloat16)
    grad_key = weight_sum[:, query_cols:query_cols + key_cols].astype(jnp.bfloat16)
    grad_value = weight_sum[:, query_cols + key_cols:].astype(jnp.bfloat16)
    return (attended, input_grad, grad_query, grad_key, grad_value)
```

```python
from functools import partial
import math

import jax
import jax.numpy as jnp
from jax import lax
from jax.experimental import pallas as pl
from jax.experimental.pallas import tpu as pltpu
from jax.sharding import PartitionSpec as P

WINDOW = 1024
TILE = 128

norm_eps = 1e-06
rope_base = 10000.0

NT = (((1,), (1,)), ((), ()))
NN = (((1,), (0,)), ((), ()))
TN = (((0,), (0,)), ((), ()))


def mm(a, b, dims):
    return lax.dot_general(a, b, dims, preferred_element_type=jnp.float32)


def shifted(block, axis, distance):
    count = lax.axis_size(axis)
    route = [(i, i + distance) for i in range(count) if 0 <= i + distance < count]
    return lax.ppermute(block, axis, route)


def rope_tables(positions, head_width):
    half_width = head_width // 2
    indices = jnp.arange(half_width, dtype=jnp.float32)
    frequency = jnp.power(rope_base, -2.0 * indices / head_width)
    angles = positions.astype(jnp.float32)[:, None] * frequency[None, :]
    return (jnp.cos(angles), jnp.sin(angles))


def rotate(vector, cosine_table, sine_table):
    half_width = vector.shape[-1] // 2
    lower = vector[..., :half_width]
    upper = vector[..., half_width:]
    return jnp.concatenate(
        [
            lower * cosine_table - upper * sine_table,
            upper * cosine_table + lower * sine_table,
        ],
        axis=-1,
    )


def normalize(vector, gain_vector):
    inv_rms = lax.rsqrt(jnp.mean(vector * vector, axis=-1, keepdims=True) + norm_eps)
    return (vector * inv_rms * gain_vector, inv_rms)


def norm_back(vector, inv_rms, gain_vector, upstream):
    scaled = upstream * gain_vector
    return inv_rms * scaled - vector * (inv_rms * inv_rms * inv_rms) * jnp.mean(
        vector * scaled, axis=-1, keepdims=True
    )


def attention_kernel(reach, heads, width, *refs):
    q_ref, go_ref, cos_ref, sin_ref, limit_ref, gain_ref = refs[:6]
    kv_refs = refs[6 : 7 + reach]
    att_ref, qg_ref = refs[7 + reach : 9 + reach]
    dkv_refs = refs[9 + reach : 10 + 2 * reach]
    kcat, vcat, dk_acc, dv_acc = refs[10 + 2 * reach :]
    tile = pl.program_id(1)
    span = WINDOW + TILE
    scale = 1.0 / math.sqrt(width)

    @pl.when(tile == 0)
    def _():
        row = 0
        for ref in kv_refs:
            rows = ref.shape[0]
            kcat[row : row + rows, :] = ref[:, :width]
            vcat[row : row + rows, :] = ref[:, width:]
            row += rows
        dk_acc[...] = jnp.zeros_like(dk_acc)
        dv_acc[...] = jnp.zeros_like(dv_acc)

    gain = gain_ref[...]
    cosine = cos_ref[...]
    sine = sin_ref[...]
    raws = [q_ref[:, h * width : (h + 1) * width] for h in range(heads)]
    states, invs = [], []
    for raw in raws:
        normed, inv = normalize(raw, gain)
        states.append((rotate(normed, cosine, sine) * scale).astype(jnp.bfloat16))
        invs.append(inv)
    q = jnp.concatenate(states, axis=0)
    go = jnp.concatenate(
        [go_ref[:, h * width : (h + 1) * width] for h in range(heads)], axis=0
    )
    start = pl.multiple_of(tile * TILE, TILE)
    k = kcat[pl.ds(start, span), :]
    v = vcat[pl.ds(start, span), :]
    scores = mm(q, k, NT)
    distance = (
        WINDOW
        + lax.broadcasted_iota(jnp.int32, (TILE, span), 0)
        - lax.broadcasted_iota(jnp.int32, (TILE, span), 1)
    )
    visible = (distance >= 0) & (distance <= limit_ref[...])
    bias = jnp.where(visible, 0.0, -jnp.inf)
    scores = scores + jnp.concatenate([bias] * heads, axis=0)
    peak = jnp.max(scores, axis=-1, keepdims=True)
    weights = jnp.exp(scores - peak)
    total = jnp.sum(weights, axis=-1, keepdims=True)
    probs = weights * (1.0 / total)
    probs_bf = probs.astype(jnp.bfloat16)
    attended = mm(probs_bf, v, NN).astype(jnp.bfloat16)
    for h in range(heads):
        att_ref[:, h * width : (h + 1) * width] = attended[h * TILE : (h + 1) * TILE]
    delta = jnp.sum(
        go.astype(jnp.float32) * attended.astype(jnp.float32), axis=-1, keepdims=True
    )
    dprobs = mm(go, v, NT)
    dscores = (probs * (dprobs - delta)).astype(jnp.bfloat16)
    dq = mm(dscores, k, NN)
    dk_acc[pl.ds(start, span), :] += mm(dscores, q, TN)
    dv_acc[pl.ds(start, span), :] += mm(probs_bf, go, TN)
    for h in range(heads):
        up = rotate(dq[h * TILE : (h + 1) * TILE], cosine, -sine) * scale
        qg_ref[:, h * width : (h + 1) * width] = norm_back(
            raws[h], invs[h], gain, up
        ).astype(jnp.bfloat16)

    @pl.when(tile == pl.num_programs(1) - 1)
    def _():
        row = 0
        for ref in dkv_refs:
            rows = ref.shape[0]
            ref[:, :width] = dk_acc[row : row + rows, :].astype(ref.dtype)
            ref[:, width:] = dv_acc[row : row + rows, :].astype(ref.dtype)
            row += rows


def attention(q_raw, out_grad, cosine, sine, limit, gain, kv_blocks, groups):
    row_count, columns = q_raw.shape
    width = gain.shape[-1]
    heads = columns // groups // width
    reach = len(kv_blocks) - 1
    own = pl.BlockSpec((TILE, heads * width), lambda g, t: (t, g))
    table = pl.BlockSpec((TILE, width // 2), lambda g, t: (t, 0))
    kv_specs = [
        pl.BlockSpec((block.shape[0], 2 * width), lambda g, t: (0, g)) for block in kv_blocks
    ]
    keys = WINDOW + row_count
    flops = 6 * 2 * row_count * heads * groups * (WINDOW + TILE) * width
    return pl.pallas_call(
        partial(attention_kernel, reach, heads, width),
        grid=(groups, row_count // TILE),
        in_specs=[
            own,
            own,
            table,
            table,
            pl.BlockSpec((TILE, 1), lambda g, t: (t, 0)),
            pl.BlockSpec((1, width), lambda g, t: (0, 0)),
        ]
        + kv_specs,
        out_specs=[own, own] + kv_specs,
        out_shape=[
            jax.ShapeDtypeStruct((row_count, columns), jnp.bfloat16),
            jax.ShapeDtypeStruct((row_count, columns), jnp.bfloat16),
        ]
        + [
            jax.ShapeDtypeStruct(block.shape, jnp.bfloat16 if i < reach else jnp.float32)
            for i, block in enumerate(kv_blocks)
        ],
        scratch_shapes=[
            pltpu.VMEM((keys, width), jnp.bfloat16),
            pltpu.VMEM((keys, width), jnp.bfloat16),
            pltpu.VMEM((keys, width), jnp.float32),
            pltpu.VMEM((keys, width), jnp.float32),
        ],
        compiler_params=pltpu.CompilerParams(vmem_limit_bytes=40 * 1024 * 1024),
        cost_estimate=pl.CostEstimate(
            flops=flops, bytes_accessed=16 * 1024 * 1024, transcendentals=2 * 1024 * 1024
        ),
    )(q_raw, out_grad, cosine, sine, limit, gain, *kv_blocks)


def head_sum(terms, axis):
    count = lax.axis_size(axis)
    me = lax.axis_index(axis)
    pieces = terms.reshape(count, terms.shape[0] // count, terms.shape[1])
    total = lax.dynamic_index_in_dim(pieces, me, 0, keepdims=False).astype(jnp.float32)
    for distance in range(1, count):
        piece = lax.dynamic_index_in_dim(
            pieces, lax.rem(me + distance, count), 0, keepdims=False
        )
        got = lax.ppermute(piece, axis, [(i, (i + distance) % count) for i in range(count)])
        total = total + got.astype(jnp.float32)
    return total.astype(jnp.bfloat16)


def on_device(tokens, w_query, w_key, w_value, query_gain, key_gain, positions, out_grad):
    gathered = lax.all_gather(tokens, "head", axis=0, tiled=True)
    row_count, model_width = gathered.shape
    width = query_gain.shape[0]
    groups = w_key.shape[1] // width
    rank_count = lax.axis_size("ctx")
    head_ranks = lax.axis_size("head")
    my_rank = lax.axis_index("ctx")
    reach = (WINDOW + row_count - 1) // row_count
    sub_rows = tokens.shape[0]
    out_rows = model_width // rank_count

    value_states = mm(gathered, w_value, NN).astype(jnp.bfloat16)
    key_raw = mm(gathered, w_key, NN).reshape(row_count, groups, width)
    cosine, sine = rope_tables(positions, width)
    key_normed, key_inv = normalize(key_raw, key_gain)
    key_states = rotate(key_normed, cosine[:, None, :], sine[:, None, :]).astype(jnp.bfloat16)
    value_parts = value_states.reshape(row_count, groups, width)
    local_kv = jnp.concatenate([key_states, value_parts], axis=-1).reshape(
        row_count, groups * 2 * width
    )
    skipped = [max(0, stride * row_count - WINDOW) for stride in range(reach + 1)]
    kv_blocks = [
        shifted(local_kv[skipped[stride] :], "ctx", stride) for stride in range(reach, 0, -1)
    ] + [local_kv]

    query_raw = mm(gathered, w_query, NN)
    rows = jnp.arange(row_count, dtype=jnp.int32)
    limit = jnp.minimum(jnp.minimum(positions, WINDOW - 1), my_rank * row_count + rows)[:, None]
    attended, query_raw_grad, *dkv = attention(
        query_raw, out_grad, cosine, sine, limit, query_gain[None, :], kv_blocks, groups
    )

    stripes = [list(range(first, rank_count, 2)) for first in range(2)]
    pairs = rank_count // 2
    spread = lax.all_to_all(
        tokens.reshape(sub_rows, pairs, 2 * out_rows).swapaxes(0, 1),
        "ctx",
        0,
        0,
        axis_index_groups=stripes,
    )
    columns = lax.all_gather(spread, "head", axis=1, tiled=True)
    columns = columns.reshape(pairs * row_count, 2, out_rows)
    side = lax.rem(my_rank, 2)
    own_columns = lax.dynamic_index_in_dim(columns, side, 1, keepdims=False)
    pair_columns = lax.dynamic_index_in_dim(columns, 1 - side, 1, keepdims=False)
    swap = [(i, i + 1 - 2 * (i % 2)) for i in range(rank_count)]

    def weight_grad(grads):
        sent = mm(pair_columns, grads, TN).astype(jnp.bfloat16)
        got = lax.ppermute(sent, "ctx", swap)
        return (mm(own_columns, grads, TN) + got.astype(jnp.float32)).astype(jnp.bfloat16)

    query_all = lax.all_gather(
        query_raw_grad, "ctx", axis=0, tiled=True, axis_index_groups=stripes
    )

    dkv_sum = dkv[reach]
    for stride in range(1, reach + 1):
        back = shifted(dkv[reach - stride], "ctx", -stride).astype(jnp.float32)
        dkv_sum = dkv_sum + jnp.pad(back, ((skipped[stride], 0), (0, 0)))
    dkv_parts = dkv_sum.reshape(row_count, groups, 2 * width)
    key_raw_grad = (
        norm_back(
            key_raw,
            key_inv,
            key_gain,
            rotate(dkv_parts[..., :width], cosine[:, None, :], -sine[:, None, :]),
        )
        .astype(jnp.bfloat16)
        .reshape(row_count, groups * width)
    )
    value_grads = dkv_parts[..., width:].astype(jnp.bfloat16).reshape(row_count, groups * width)
    kv_all = lax.all_gather(
        jnp.concatenate([key_raw_grad, value_grads], axis=1),
        "ctx",
        axis=0,
        tiled=True,
        axis_index_groups=stripes,
    )
    input_terms = (
        mm(query_raw_grad, w_query, NT)
        + mm(key_raw_grad, w_key, NT)
        + mm(value_grads, w_value, NT)
    )
    input_grad = head_sum(input_terms.astype(jnp.bfloat16), "head")
    grad_query = weight_grad(query_all)
    grad_kv = weight_grad(kv_all)
    key_cols = groups * width
    return (
        attended,
        input_grad,
        grad_query,
        grad_kv[:, :key_cols],
        grad_kv[:, key_cols:],
    )


def solution(mesh):
    in_specs = (
        P(("ctx", "head"), None),
        P(None, "head"),
        P(None, "head"),
        P(None, "head"),
        P(),
        P(),
        P("ctx"),
        P("ctx", "head"),
    )
    out_specs = (
        P("ctx", "head"),
        P(("ctx", "head"), None),
        P("ctx", "head"),
        P("ctx", "head"),
        P("ctx", "head"),
    )
    return jax.shard_map(
        on_device, mesh=mesh, in_specs=in_specs, out_specs=out_specs, check_vma=False
    )
```

```python
from functools import partial
import math

import jax
import jax.numpy as jnp
from jax import lax
from jax.experimental import pallas as pl
from jax.experimental.pallas import tpu as pltpu
from jax.sharding import PartitionSpec as P

WINDOW = 1024
TILE = 128

norm_eps = 1e-06
rope_base = 10000.0

NT = (((1,), (1,)), ((), ()))
NN = (((1,), (0,)), ((), ()))
TN = (((0,), (0,)), ((), ()))


def mm(a, b, dims):
    return lax.dot_general(a, b, dims, preferred_element_type=jnp.float32)


def shifted(block, axis, distance):
    count = lax.axis_size(axis)
    route = [(i, i + distance) for i in range(count) if 0 <= i + distance < count]
    return lax.ppermute(block, axis, route)


def rope_tables(positions, head_width):
    half_width = head_width // 2
    indices = jnp.arange(half_width, dtype=jnp.float32)
    frequency = jnp.power(rope_base, -2.0 * indices / head_width)
    angles = positions.astype(jnp.float32)[:, None] * frequency[None, :]
    return (jnp.cos(angles), jnp.sin(angles))


def rotate(vector, cosine_table, sine_table):
    half_width = vector.shape[-1] // 2
    lower = vector[..., :half_width]
    upper = vector[..., half_width:]
    return jnp.concatenate(
        [
            lower * cosine_table - upper * sine_table,
            upper * cosine_table + lower * sine_table,
        ],
        axis=-1,
    )


def normalize(vector, gain_vector):
    inv_rms = lax.rsqrt(jnp.mean(vector * vector, axis=-1, keepdims=True) + norm_eps)
    return (vector * inv_rms * gain_vector, inv_rms)


def norm_back(vector, inv_rms, gain_vector, upstream):
    scaled = upstream * gain_vector
    return inv_rms * scaled - vector * (inv_rms * inv_rms * inv_rms) * jnp.mean(
        vector * scaled, axis=-1, keepdims=True
    )


def attention_kernel(reach, heads, width, *refs):
    q_ref, go_ref, cos_ref, sin_ref, limit_ref, gain_ref = refs[:6]
    kv_refs = refs[6 : 7 + reach]
    att_ref, qg_ref = refs[7 + reach : 9 + reach]
    dkv_refs = refs[9 + reach : 10 + 2 * reach]
    kcat, vcat, dk_acc, dv_acc = refs[10 + 2 * reach :]
    tile = pl.program_id(1)
    span = WINDOW + TILE
    scale = 1.0 / math.sqrt(width)

    @pl.when(tile == 0)
    def _():
        row = 0
        for ref in kv_refs:
            rows = ref.shape[0]
            kcat[row : row + rows, :] = ref[:, :width]
            vcat[row : row + rows, :] = ref[:, width:]
            row += rows
        dk_acc[...] = jnp.zeros_like(dk_acc)
        dv_acc[...] = jnp.zeros_like(dv_acc)

    gain = gain_ref[...]
    cosine = cos_ref[...]
    sine = sin_ref[...]
    raws = [q_ref[:, h * width : (h + 1) * width] for h in range(heads)]
    states, invs = [], []
    for raw in raws:
        normed, inv = normalize(raw, gain)
        states.append((rotate(normed, cosine, sine) * scale).astype(jnp.bfloat16))
        invs.append(inv)
    q = jnp.concatenate(states, axis=0)
    go = jnp.concatenate(
        [go_ref[:, h * width : (h + 1) * width] for h in range(heads)], axis=0
    )
    start = pl.multiple_of(tile * TILE, TILE)
    k = kcat[pl.ds(start, span), :]
    v = vcat[pl.ds(start, span), :]
    scores = mm(q, k, NT)
    distance = (
        WINDOW
        + lax.broadcasted_iota(jnp.int32, (TILE, span), 0)
        - lax.broadcasted_iota(jnp.int32, (TILE, span), 1)
    )
    visible = (distance >= 0) & (distance <= limit_ref[...])
    bias = jnp.where(visible, 0.0, -jnp.inf)
    scores = scores + jnp.concatenate([bias] * heads, axis=0)
    peak = jnp.max(scores, axis=-1, keepdims=True)
    weights = jnp.exp(scores - peak)
    total = jnp.sum(weights, axis=-1, keepdims=True)
    probs = weights * (1.0 / total)
    probs_bf = probs.astype(jnp.bfloat16)
    attended = mm(probs_bf, v, NN).astype(jnp.bfloat16)
    for h in range(heads):
        att_ref[:, h * width : (h + 1) * width] = attended[h * TILE : (h + 1) * TILE]
    delta = jnp.sum(
        go.astype(jnp.float32) * attended.astype(jnp.float32), axis=-1, keepdims=True
    )
    dprobs = mm(go, v, NT)
    dscores = (probs * (dprobs - delta)).astype(jnp.bfloat16)
    dq = mm(dscores, k, NN)
    dk_acc[pl.ds(start, span), :] += mm(dscores, q, TN)
    dv_acc[pl.ds(start, span), :] += mm(probs_bf, go, TN)
    for h in range(heads):
        up = rotate(dq[h * TILE : (h + 1) * TILE], cosine, -sine) * scale
        qg_ref[:, h * width : (h + 1) * width] = norm_back(
            raws[h], invs[h], gain, up
        ).astype(jnp.bfloat16)

    @pl.when(tile == pl.num_programs(1) - 1)
    def _():
        row = 0
        for ref in dkv_refs:
            rows = ref.shape[0]
            ref[:, :width] = dk_acc[row : row + rows, :].astype(ref.dtype)
            ref[:, width:] = dv_acc[row : row + rows, :].astype(ref.dtype)
            row += rows


def attention(q_raw, out_grad, cosine, sine, limit, gain, kv_blocks, groups):
    row_count, columns = q_raw.shape
    width = gain.shape[-1]
    heads = columns // groups // width
    reach = len(kv_blocks) - 1
    own = pl.BlockSpec((TILE, heads * width), lambda g, t: (t, g))
    table = pl.BlockSpec((TILE, width // 2), lambda g, t: (t, 0))
    kv_specs = [
        pl.BlockSpec((block.shape[0], 2 * width), lambda g, t: (0, g)) for block in kv_blocks
    ]
    keys = WINDOW + row_count
    flops = 6 * 2 * row_count * heads * groups * (WINDOW + TILE) * width
    return pl.pallas_call(
        partial(attention_kernel, reach, heads, width),
        grid=(groups, row_count // TILE),
        in_specs=[
            own,
            own,
            table,
            table,
            pl.BlockSpec((TILE, 1), lambda g, t: (t, 0)),
            pl.BlockSpec((1, width), lambda g, t: (0, 0)),
        ]
        + kv_specs,
        out_specs=[own, own] + kv_specs,
        out_shape=[
            jax.ShapeDtypeStruct((row_count, columns), jnp.bfloat16),
            jax.ShapeDtypeStruct((row_count, columns), jnp.bfloat16),
        ]
        + [
            jax.ShapeDtypeStruct(block.shape, jnp.bfloat16 if i < reach else jnp.float32)
            for i, block in enumerate(kv_blocks)
        ],
        scratch_shapes=[
            pltpu.VMEM((keys, width), jnp.bfloat16),
            pltpu.VMEM((keys, width), jnp.bfloat16),
            pltpu.VMEM((keys, width), jnp.float32),
            pltpu.VMEM((keys, width), jnp.float32),
        ],
        compiler_params=pltpu.CompilerParams(vmem_limit_bytes=40 * 1024 * 1024),
        cost_estimate=pl.CostEstimate(
            flops=flops, bytes_accessed=16 * 1024 * 1024, transcendentals=2 * 1024 * 1024
        ),
    )(q_raw, out_grad, cosine, sine, limit, gain, *kv_blocks)


def head_sum(terms, axis):
    count = lax.axis_size(axis)
    me = lax.axis_index(axis)
    pieces = terms.reshape(count, terms.shape[0] // count, terms.shape[1])
    total = lax.dynamic_index_in_dim(pieces, me, 0, keepdims=False).astype(jnp.float32)
    for distance in range(1, count):
        piece = lax.dynamic_index_in_dim(
            pieces, lax.rem(me + distance, count), 0, keepdims=False
        )
        got = lax.ppermute(piece, axis, [(i, (i + distance) % count) for i in range(count)])
        total = total + got.astype(jnp.float32)
    return total.astype(jnp.bfloat16)


def on_device(tokens, w_query, w_key, w_value, query_gain, key_gain, positions, out_grad):
    gathered = lax.all_gather(tokens, "head", axis=0, tiled=True)
    row_count, model_width = gathered.shape
    width = query_gain.shape[0]
    groups = w_key.shape[1] // width
    rank_count = lax.axis_size("ctx")
    head_ranks = lax.axis_size("head")
    my_rank = lax.axis_index("ctx")
    reach = (WINDOW + row_count - 1) // row_count
    sub_rows = tokens.shape[0]
    out_rows = model_width // rank_count

    value_states = mm(gathered, w_value, NN).astype(jnp.bfloat16)
    key_raw = mm(gathered, w_key, NN).reshape(row_count, groups, width)
    cosine, sine = rope_tables(positions, width)
    key_normed, key_inv = normalize(key_raw, key_gain)
    key_states = rotate(key_normed, cosine[:, None, :], sine[:, None, :]).astype(jnp.bfloat16)
    value_parts = value_states.reshape(row_count, groups, width)
    local_kv = jnp.concatenate([key_states, value_parts], axis=-1).reshape(
        row_count, groups * 2 * width
    )
    skipped = [max(0, stride * row_count - WINDOW) for stride in range(reach + 1)]
    kv_blocks = [
        shifted(local_kv[skipped[stride] :], "ctx", stride) for stride in range(reach, 0, -1)
    ] + [local_kv]

    query_raw = mm(gathered, w_query, NN)
    rows = jnp.arange(row_count, dtype=jnp.int32)
    limit = jnp.minimum(jnp.minimum(positions, WINDOW - 1), my_rank * row_count + rows)[:, None]
    attended, query_raw_grad, *dkv = attention(
        query_raw, out_grad, cosine, sine, limit, query_gain[None, :], kv_blocks, groups
    )

    stripes = [list(range(first, rank_count, 2)) for first in range(2)]
    pairs = rank_count // 2
    spread = lax.all_to_all(
        tokens.reshape(sub_rows, pairs, 2 * out_rows).swapaxes(0, 1),
        "ctx",
        0,
        0,
        axis_index_groups=stripes,
    )
    columns = lax.all_gather(spread, "head", axis=1, tiled=True)
    columns = columns.reshape(pairs * row_count, 2, out_rows)
    side = lax.rem(my_rank, 2)
    own_columns = lax.dynamic_index_in_dim(columns, side, 1, keepdims=False)
    pair_columns = lax.dynamic_index_in_dim(columns, 1 - side, 1, keepdims=False)
    swap = [(i, i + 1 - 2 * (i % 2)) for i in range(rank_count)]

    def weight_grad(grads, own, pair):
        sent = mm(pair, grads, TN).astype(jnp.bfloat16)
        got = lax.ppermute(sent, "ctx", swap)
        return (mm(own, grads, TN) + got.astype(jnp.float32)).astype(jnp.bfloat16)

    def around(stripe_columns):
        edge = (pairs - 1) * row_count
        padded = jnp.pad(stripe_columns, ((edge, edge), (0, 0)))
        first = lax.div(my_rank, 2) * row_count
        return lax.dynamic_slice_in_dim(padded, first, edge + pairs * row_count, 0)

    own_around, pair_around = around(own_columns), around(pair_columns)

    query_all = lax.all_gather(
        query_raw_grad, "ctx", axis=0, tiled=True, axis_index_groups=stripes
    )

    dkv_sum = dkv[reach]
    for stride in range(1, reach + 1):
        back = shifted(dkv[reach - stride], "ctx", -stride).astype(jnp.float32)
        dkv_sum = dkv_sum + jnp.pad(back, ((skipped[stride], 0), (0, 0)))
    dkv_parts = dkv_sum.reshape(row_count, groups, 2 * width)
    key_raw_grad = (
        norm_back(
            key_raw,
            key_inv,
            key_gain,
            rotate(dkv_parts[..., :width], cosine[:, None, :], -sine[:, None, :]),
        )
        .astype(jnp.bfloat16)
        .reshape(row_count, groups * width)
    )
    value_grads = dkv_parts[..., width:].astype(jnp.bfloat16).reshape(row_count, groups * width)
    upward = downward = jnp.concatenate([key_raw_grad, value_grads], axis=1)
    kv_parts = [upward]
    for step in range(1, pairs):
        upward, downward = shifted(upward, "ctx", 2), shifted(downward, "ctx", -2)
        kv_parts = [upward] + kv_parts + [downward]
    kv_all = jnp.concatenate(kv_parts, axis=0)
    input_terms = (
        mm(query_raw_grad, w_query, NT)
        + mm(key_raw_grad, w_key, NT)
        + mm(value_grads, w_value, NT)
    )
    input_grad = head_sum(input_terms.astype(jnp.bfloat16), "head")
    grad_query = weight_grad(query_all, own_columns, pair_columns)
    grad_kv = weight_grad(kv_all, own_around, pair_around)
    key_cols = groups * width
    return (
        attended,
        input_grad,
        grad_query,
        grad_kv[:, :key_cols],
        grad_kv[:, key_cols:],
    )


def solution(mesh):
    in_specs = (
        P(("ctx", "head"), None),
        P(None, "head"),
        P(None, "head"),
        P(None, "head"),
        P(),
        P(),
        P("ctx"),
        P("ctx", "head"),
    )
    out_specs = (
        P("ctx", "head"),
        P(("ctx", "head"), None),
        P("ctx", "head"),
        P("ctx", "head"),
        P("ctx", "head"),
    )
    return jax.shard_map(
        on_device, mesh=mesh, in_specs=in_specs, out_specs=out_specs, check_vma=False
    )
```
